32 devices in a mesh: parts: 2 (over y), rows: 16 (over z, x, core).
Axes of the slice: x: 2, y: 2, z: 4, core: 2. Of those that a mesh axis runs over, the one named last changes fastest.
Arguments:
- factor_panels: float32 [16384, 1536], P(('parts', 'rows')), parts along dimension 0, as said below
- targets: float32 [16384, 256], P(('parts', 'rows')), parts along dimension 0, may hold values from -6 to 6
- later_solutions: float32 [16384, 256], P(('parts', 'rows')), parts along dimension 0, as said below
Outputs:
- solved_rows: float32 [16384, 256], P(('parts', 'rows')), parts along dimension 0
The draws below stay inside these ranges and needn't reach their ends.
There are 2 independent parts, one for each index of `parts`. The reference program is written for one: setup_inputs(seed, part) draws one part's arguments, and reference() takes and returns one part's arrays. A program takes and returns all parts, laid end to end along the dimension named above; each array names one. Nothing has to cross between parts.
Inputs may be any that keep to these rules, and one draw needn't show every extreme that they name: `factor_panels`: in rows of block d < 3, column blocks above d are zero and column block d holds a lower-triangular inverse diagonal block. `later_solutions`: the first 1536 rows are zero.
All inputs are finite; a program needn't handle non-finite values.
Results may differ from the reference program's by a relative error of at most 0.0001.
Values sent between devices are 32-bit elements; how exact they have to be, the bound alone decides.
A program may use at most 64 MiB of HBM per device.

```python
import math
import jax
import jax.numpy as jnp
from jax import lax

BLK = 512
PANELS = 3
NRHS = 256
NN = 8192


def draw_factor_panels(key, part):
    width = PANELS * BLK
    row_index = jnp.arange(NN, dtype=jnp.int32)[:, None]
    column_index = jnp.arange(width, dtype=jnp.int32)[None, :]
    row_block = row_index // BLK
    column_block = column_index // BLK
    normal_part = jax.random.normal(jax.random.fold_in(key, 11), (NN, width), jnp.float32)
    diagonal_part = jax.random.uniform(jax.random.fold_in(key, 12), (NN, width), jnp.float32, 0.6, 1.4)
    strictly_lower = column_index % BLK < row_index % BLK
    on_diagonal = column_index % BLK == row_index % BLK
    inverse_block = jnp.where(strictly_lower, 0.5 / math.sqrt(BLK) * normal_part, jnp.where(on_diagonal, diagonal_part, 0.0))
    window_entries = jnp.where(column_block < row_block, 0.7 / math.sqrt(BLK) * normal_part, jnp.where(column_block == row_block, inverse_block, 0.0))
    later_entries = normal_part / math.sqrt(width)
    return jnp.where(row_block < PANELS, window_entries, later_entries).astype(jnp.float32)


def draw_later_solutions(key, part):
    width = PANELS * BLK
    normal_part = jax.random.normal(jax.random.fold_in(key, 21), (NN, NRHS), jnp.float32)
    row_index = jnp.arange(NN, dtype=jnp.int32)[:, None]
    scaled = normal_part * math.sqrt(width / NN)
    return jnp.where(row_index < width, 0.0, scaled).astype(jnp.float32)


def shard_levels(stream_key, extent, cuts, low, top_value):
    def one(dim, shards_of):
        heights = jax.random.uniform(jax.random.fold_in(jax.random.fold_in(stream_key, 6), dim), (shards_of,), jnp.float32, low / len(cuts), top_value / len(cuts))
        return jnp.repeat(jnp.exp(heights), extent[dim] // shards_of).reshape((-1,) + (1,) * (len(extent) - dim - 1))

    level = one(*cuts[0])
    for cut in cuts[1:]:
        level = level * one(*cut)
    return level


def centred(stream_key, dims, deviation, bound, shards=(), kind=jnp.bfloat16):
    gain = shard_levels(stream_key, dims, shards, -0.22, 0.18) if shards else 1.0
    array = jax.random.normal(stream_key, dims, jnp.float32) * deviation * gain
    return jnp.minimum(jnp.maximum(array, -bound), bound).astype(kind)


def setup_inputs(seed: int = 0, part: int = 0) -> dict:
    splits = jax.random.split(jax.random.key(seed), 4)
    part_keys = jax.random.split(jax.random.fold_in(splits[3], part), 4)
    return {
        "factor_panels": draw_factor_panels(jax.random.fold_in(jax.random.fold_in(splits[3], part), 71), part),
        "targets": centred(part_keys[1], (NN, NRHS), 1.0, 6.0, ((0, 16),), jnp.float32),
        "later_solutions": draw_later_solutions(jax.random.fold_in(jax.random.fold_in(splits[3], part), 71), part),
    }


def reference(factor_panels, targets, later_solutions):
    exact_mode = lax.Precision.HIGHEST
    width = PANELS * BLK
    residual = targets
    forward_parts = []
    for panel in range(PANELS):
        start = panel * BLK
        stop = start + BLK
        forward_part = jnp.dot(factor_panels[start:stop, start:stop], residual[start:stop], precision=exact_mode, preferred_element_type=jnp.float32)
        forward_parts.append(forward_part)
        update = jnp.dot(factor_panels[stop:, start:stop], forward_part, precision=exact_mode, preferred_element_type=jnp.float32)
        residual = jnp.concatenate([residual[:stop], residual[stop:] - update], axis=0)
    known = later_solutions
    for panel in reversed(range(PANELS)):
        start = panel * BLK
        stop = start + BLK
        fan_sum = jnp.dot(factor_panels[stop:, start:stop].T, known[stop:], precision=exact_mode, preferred_element_type=jnp.float32)
        back_part = jnp.dot(factor_panels[start:stop, start:stop].T, forward_parts[panel] - fan_sum, precision=exact_mode, preferred_element_type=jnp.float32)
        known = jnp.concatenate([known[:start], back_part, known[stop:]], axis=0)
    return jnp.concatenate([known[:width], residual[width:]], axis=0)
```

```python
import functools

import jax
import jax.numpy as jnp
from jax import lax
from jax.experimental import pallas as pl
from jax.experimental.pallas import tpu as pltpu
from jax.sharding import PartitionSpec as P

MESH = pl.DeviceIdType.MESH
PLANE = 4
SUBS = 2
GROUPS = 2


def split(value):
    high = value.astype(jnp.bfloat16)
    return high, (value - high.astype(jnp.float32)).astype(jnp.bfloat16)


def triple(left, right, contract):
    def one(a, b):
        return lax.dot_general(
            a, b, (((1,), (contract,)), ((), ())), preferred_element_type=jnp.float32
        )

    return one(left[0], right[0]) + (one(left[0], right[1]) + one(left[1], right[0]))


def kernel(
    devices, panels,
    p_hbm, t_hbm, later_hbm, out_ref,
    p_ref, t_ref, later_ref, p_high, p_low,
    y_ref, term, from_core, from_x, from_z, part_x, part_z, fan, send_w, got_w,
    in_sem, send_sem, y_sem, core_sem, x_sem, z_sem, fan_sem, w_sem,
):
    block, rhs = t_ref.shape
    levels = devices // PLANE
    piece = rhs // PLANE // SUBS
    group = rhs // GROUPS
    me = lax.axis_index("rows")
    level, q = me // PLANE, me % PLANE
    x, core = q // 2, q % 2
    mine = core * 2 + x
    facing = core * 2 + 1 - x
    sibling = me + 1 - 2 * core
    across = me + 2 - 4 * x
    up, down = me - PLANE, me + PLANE

    loads = {"t": pltpu.make_async_copy(t_hbm, t_ref, in_sem.at[0])}
    loads["later"] = pltpu.make_async_copy(later_hbm, later_ref, in_sem.at[1])
    for k in range(panels):
        loads[k] = pltpu.make_async_copy(
            p_hbm.at[:, k * block : (k + 1) * block], p_ref.at[k], in_sem.at[2 + k]
        )
    for name in ["t", 0, "later"] + list(range(panels - 1, 0, -1)):
        loads[name].start()

    barrier = pltpu.get_barrier_semaphore()
    for step in range(1, PLANE):
        other = level * PLANE + (q + step) % PLANE
        pl.semaphore_signal(barrier, inc=1, device_id={"rows": other}, device_id_type=MESH)

    @pl.when(level > 0)
    def _():
        pl.semaphore_signal(barrier, inc=1, device_id={"rows": up}, device_id_type=MESH)

    @pl.when(level < levels - 1)
    def _():
        pl.semaphore_signal(barrier, inc=1, device_id={"rows": down}, device_id_type=MESH)

    inner = jnp.logical_and(level > 0, level < levels - 1)

    @pl.when(inner)
    def _():
        pl.semaphore_wait(barrier, PLANE + 1)

    @pl.when(jnp.logical_not(inner))
    def _():
        pl.semaphore_wait(barrier, PLANE)

    class Sends:
        def __init__(self):
            self.held = []

        def __call__(self, src, dst, recv, device, when=None):
            copy = pltpu.make_async_remote_copy(
                src_ref=src, dst_ref=dst, send_sem=send_sem.at[len(self.held)], recv_sem=recv,
                device_id={"rows": device}, device_id_type=MESH,
            )
            self.held.append((copy, when))
            if when is None:
                copy.start()
            else:
                pl.when(when)(copy.start)

        def finish(self):
            for copy, when in self.held:
                if when is None:
                    copy.wait_send()
                else:
                    pl.when(when)(copy.wait_send)

    def arrive(ref, sem):
        pltpu.make_async_remote_copy(
            src_ref=ref, dst_ref=ref, send_sem=send_sem.at[0], recv_sem=sem,
            device_id={"rows": sibling}, device_id_type=MESH,
        ).wait_recv()

    def send_y(send, k, at, h, device, when=None):
        send(y_ref.at[k, at, h], y_ref.at[k, at, h], y_sem.at[k, at, h], device, when)

    def wait_y(k, at, h):
        arrive(y_ref.at[k, at, h], y_sem.at[k, at, h])

    def y_value(k, g=None):
        value = y_ref[k].reshape(rhs, block)
        return value if g is None else value[g * group : (g + 1) * group]

    def y_group(k, g):
        per = PLANE // GROUPS
        return y_ref[k, g * per : (g + 1) * per].reshape(group, block)

    def fan_group(g):
        per = PLANE // GROUPS
        return fan[g * per : (g + 1) * per].reshape(group, block)

    def store_y(k, g, value):
        per = PLANE // GROUPS
        y_ref[k, g * per : (g + 1) * per] = value.reshape(per, SUBS, piece, block)

    def load_panel(k):
        loads[k].wait()
        high, low = split(p_ref[k])
        p_high[k] = high
        p_low[k] = low

    def panel(k):
        return p_high[k], p_low[k]

    def in_group(g):
        per = PLANE // GROUPS
        return range(g * per, (g + 1) * per)

    def rows_of(g):
        return pl.ds(g * group, group)

    def relay(send, k, owner_is_me, own_term):
        for h in range(SUBS):
            if own_term:
                value = term[k, mine, h]
            else:
                arrive(from_x.at[k, h], x_sem.at[k, h])
                value = from_x[k, h]
            arrive(from_z.at[k, h], z_sem.at[k, h])
            value = value + from_z[k, h]
            if owner_is_me:
                fan[mine, h] = value
            else:
                part_z[k, h] = value
                send(part_z.at[k, h], fan.at[mine, h], fan_sem.at[mine, h], k)

    def fan_wait(owner, g):
        own = (owner % 2) * 2 + owner // 2
        for at in in_group(g):
            if at != own:
                for h in range(SUBS):
                    arrive(fan.at[at, h], fan_sem.at[at, h])

    def send_w_group(send, slot, to_slot, g, device):
        send(send_w.at[slot, rows_of(g)], got_w.at[to_slot, rows_of(g)], w_sem.at[to_slot, g], device)

    def wait_w(slot, g):
        arrive(got_w.at[slot, rows_of(g)], w_sem.at[slot, g])

    def drain(names):
        for name in names:
            loads[name].wait()

    @pl.when(me == 0)
    def _():
        send = Sends()
        loads["t"].wait()
        load_panel(0)
        target = t_ref[...].T
        for g in range(GROUPS):
            store_y(0, g, triple(split(target[g * group : (g + 1) * group]), panel(0), 1))
            for at in in_group(g):
                for h in range(SUBS):
                    send_y(send, 0, at, h, 1)
                    send_y(send, 0, at, h, 2)
                    if at == 0:
                        send_y(send, 0, at, h, PLANE)
        drain(["later", 1, 2])
        for h in range(SUBS):
            wait_y(1, 0, h)
            send_y(send, 1, 0, h, PLANE)
        relay(send, 2, False, False)
        relay(send, 1, False, False)
        for h in range(SUBS):
            wait_y(2, 0, h)
            send_y(send, 2, 0, h, PLANE)
        relay(send, 0, True, False)
        for g in range(GROUPS):
            fan_wait(0, g)
            wait_w(0, g)
            right = y_group(0, g) - fan_group(g) - got_w[0, rows_of(g)]
            wait_w(1, g)
            answer = triple(split(right - got_w[1, rows_of(g)]), panel(0), 0)
            out_ref[:, g * group : (g + 1) * group] = answer.T
        send.finish()

    @pl.when(me == 1)
    def _():
        send = Sends()
        loads["t"].wait()
        target = t_ref[...].T
        load_panel(0)
        load_panel(1)
        for g in range(GROUPS):
            for at in in_group(g):
                for h in range(SUBS):
                    wait_y(0, at, h)
                    if at == 2:
                        send_y(send, 0, at, h, 1 + PLANE)
            right = target[g * group : (g + 1) * group] - triple(split(y_group(0, g)), panel(0), 1)
            store_y(1, g, triple(split(right), panel(1), 1))
            for at in in_group(g):
                for h in range(SUBS):
                    send_y(send, 1, at, h, 2)
                    if at == 2:
                        send_y(send, 1, at, h, 1 + PLANE)
                    if at == 0:
                        send_y(send, 1, at, h, 0)
        drain(["later", 2])
        relay(send, 2, False, False)
        relay(send, 1, True, False)
        for h in range(SUBS):
            wait_y(2, 2, h)
            send_y(send, 2, 2, h, 1 + PLANE)
        relay(send, 0, False, False)
        for g in range(GROUPS):
            fan_wait(1, g)
            right = y_group(1, g) - fan_group(g)
            wait_w(0, g)
            answer = triple(split(right - got_w[0, rows_of(g)]), panel(1), 0)
            send_w[0, rows_of(g)] = triple(split(answer), panel(0), 0)
            send_w_group(send, 0, 1, g, 0)
            out_ref[:, g * group : (g + 1) * group] = answer.T
        send.finish()

    @pl.when(me == 2)
    def _():
        send = Sends()
        loads["t"].wait()
        target = t_ref[...].T
        for k in range(panels):
            load_panel(k)
        for g in range(GROUPS):
            right = target[g * group : (g + 1) * group]
            for k in range(2):
                for at in in_group(g):
                    for h in range(SUBS):
                        wait_y(k, at, h)
                        send_y(send, k, at, h, 3)
                        if at == 1:
                            send_y(send, k, at, h, 2 + PLANE)
                right = right - triple(split(y_group(k, g)), panel(k), 1)
            store_y(2, g, triple(split(right), panel(2), 1))
            for at in in_group(g):
                for h in range(SUBS):
                    if at == 0:
                        send_y(send, 2, at, h, 0)
                    if at == 1:
                        send_y(send, 2, at, h, 2 + PLANE)
                    if at == 2:
                        send_y(send, 2, at, h, 1)
                    send_y(send, 2, at, h, 3)
        drain(["later"])
        relay(send, 2, True, False)
        for g in range(GROUPS):
            fan_wait(2, g)
            answer = triple(split(y_group(2, g) - fan_group(g)), panel(2), 0)
            send_w[0, rows_of(g)] = triple(split(answer), panel(1), 0)
            send_w_group(send, 0, 0, g, 1)
            if g == 0:
                relay(send, 1, False, False)
            send_w[1, rows_of(g)] = triple(split(answer), panel(0), 0)
            send_w_group(send, 1, 0, g, 0)
            out_ref[:, g * group : (g + 1) * group] = answer.T
        relay(send, 0, False, False)
        send.finish()

    @pl.when(me >= 3)
    def _():
        plane0 = level == 0
        loads["later"].wait()
        later = split(later_ref[...].T)

        def make_term(k):
            load_panel(k)
            term[k] = triple(later, panel(k), 0).reshape(PLANE, SUBS, piece, block)

        def subtract(k):
            value = triple(panel(k), split(y_value(k)), 1)
            out_ref[...] = (t_ref[...] if k == 0 else out_ref[...]) - value

        @pl.when(plane0)
        def _():
            send = Sends()
            for k in range(panels - 1, -1, -1):
                make_term(k)
                for at, device in ((0, 0), (2, 1), (1, 2)):
                    for h in range(SUBS):
                        send(term.at[k, at, h], from_x.at[k, h], x_sem.at[k, h], device)
            loads["t"].wait()

            def take(k):
                for at in range(PLANE):
                    for h in range(SUBS):
                        wait_y(k, at, h)
                        if at == 3:
                            send_y(send, k, at, h, 3 + PLANE)

            take(0)
            take(1)
            relay(send, 2, False, True)
            relay(send, 1, False, True)
            subtract(0)
            subtract(1)
            take(2)
            relay(send, 0, False, True)
            subtract(2)
            send.finish()

        @pl.when(jnp.logical_not(plane0))
        def _():
            far = level == levels - 1
            not_far = jnp.logical_not(far)
            send = Sends()
            for k in range(panels - 1, -1, -1):
                make_term(k)
                for side in range(2):
                    for h in range(SUBS):
                        send(
                            term.at[k, (1 - core) * 2 + side, h], from_core.at[k, side, h],
                            core_sem.at[k, side, h], sibling,
                        )
            for k in range(panels - 1, -1, -1):
                for h in range(SUBS):
                    for side in range(2):
                        arrive(from_core.at[k, side, h], core_sem.at[k, side, h])
                    part_x[k, h] = term[k, facing, h] + from_core[k, 1 - x, h]
                    send(part_x.at[k, h], from_x.at[k, h], x_sem.at[k, h], across)
            loads["t"].wait()

            def line_sum(k, send):
                for h in range(SUBS):
                    arrive(from_x.at[k, h], x_sem.at[k, h])
                    part_z[k, h] = term[k, mine, h] + from_core[k, x, h] + from_x[k, h]

                    @pl.when(not_far)
                    def _():
                        arrive(from_z.at[k, h], z_sem.at[k, h])
                        part_z[k, h] += from_z[k, h]

                    send(part_z.at[k, h], from_z.at[k, h], z_sem.at[k, h], up)

            def take(k, send):
                for h in range(SUBS):
                    wait_y(k, mine, h)
                    send_y(send, k, mine, h, down, not_far)
                    send_y(send, k, mine, h, across)
                    send_y(send, k, mine, h, sibling)

            def pass_on(k, send):
                for h in range(SUBS):
                    wait_y(k, facing, h)
                    send_y(send, k, facing, h, sibling)

            def rest(k):
                for side in range(2):
                    for h in range(SUBS):
                        wait_y(k, (1 - core) * 2 + side, h)

            def middle(order):
                inner_send = Sends()
                inner_send.held = list(send.held)
                done = len(send.held)
                for step, k in order:
                    step(k, inner_send)
                inner_send.held = inner_send.held[done:]
                inner_send.finish()

            steps = {
                "near": [(take, 0), (pass_on, 0), (take, 1), (pass_on, 1), (line_sum, 2), (line_sum, 1), (line_sum, 0)],
                "far": [(line_sum, 2), (line_sum, 1), (line_sum, 0), (take, 0), (pass_on, 0), (take, 1), (pass_on, 1)],
                "mid": [(line_sum, 2), (take, 0), (line_sum, 1), (pass_on, 0), (take, 1), (line_sum, 0), (pass_on, 1)],
            }
            is_near = jnp.logical_and(level == 1, not_far)
            pl.when(is_near)(lambda: middle(steps["near"]))
            pl.when(far)(lambda: middle(steps["far"]))
            pl.when(jnp.logical_and(level > 1, not_far))(lambda: middle(steps["mid"]))
            for k in range(2):
                rest(k)
                subtract(k)
            take(2, send)
            pass_on(2, send)
            rest(2)
            subtract(2)
            send.finish()


def solution(mesh):
    devices = mesh.shape["rows"]

    def local(factor_panels, targets, later_solutions):
        block, rhs = targets.shape
        panels = factor_panels.shape[1] // block
        piece = rhs // PLANE // SUBS
        dma = pltpu.SemaphoreType.DMA
        f32 = jnp.float32
        return pl.pallas_call(
            functools.partial(kernel, devices, panels),
            out_shape=jax.ShapeDtypeStruct((block, rhs), f32),
            in_specs=[pl.BlockSpec(memory_space=pl.ANY)] * 3,
            out_specs=pl.BlockSpec(memory_space=pltpu.VMEM),
            scratch_shapes=[
                pltpu.VMEM((panels, block, block), f32),
                pltpu.VMEM((block, rhs), f32),
                pltpu.VMEM((block, rhs), f32),
                pltpu.VMEM((panels, block, block), jnp.bfloat16),
                pltpu.VMEM((panels, block, block), jnp.bfloat16),
                pltpu.VMEM((panels, PLANE, SUBS, piece, block), f32),
                pltpu.VMEM((panels, PLANE, SUBS, piece, block), f32),
                pltpu.VMEM((panels, 2, SUBS, piece, block), f32),
                pltpu.VMEM((panels, SUBS, piece, block), f32),
                pltpu.VMEM((panels, SUBS, piece, block), f32),
                pltpu.VMEM((panels, SUBS, piece, block), f32),
                pltpu.VMEM((panels, SUBS, piece, block), f32),
                pltpu.VMEM((PLANE, SUBS, piece, block), f32),
                pltpu.VMEM((2, rhs, block), f32),
                pltpu.VMEM((2, rhs, block), f32),
                dma((2 + panels,)),
                dma((128,)),
                dma((panels, PLANE, SUBS)),
                dma((panels, 2, SUBS)),
                dma((panels, SUBS)),
                dma((panels, SUBS)),
                dma((PLANE, SUBS)),
                dma((2, GROUPS)),
            ],
            compiler_params=pltpu.CompilerParams(
                collective_id=0, has_side_effects=True, vmem_limit_bytes=48 * 1024 * 1024
            ),
        )(factor_panels, targets, later_solutions)

    rows = P(("parts", "rows"), None)
    return jax.shard_map(
        local, mesh=mesh, in_specs=(rows, rows, rows), out_specs=rows, check_vma=False
    )
```

```python
import functools

import jax
import jax.numpy as jnp
from jax import lax
from jax.experimental import pallas as pl
from jax.experimental.pallas import tpu as pltpu
from jax.sharding import PartitionSpec as P

MESH = pl.DeviceIdType.MESH
PLANE = 4
SUBS = 2
GROUPS = SUBS


def split(value):
    high = value.astype(jnp.bfloat16)
    return high, (value - high.astype(jnp.float32)).astype(jnp.bfloat16)


def triple(left, right, contract):
    def one(a, b):
        return lax.dot_general(
            a, b, (((1,), (contract,)), ((), ())), preferred_element_type=jnp.float32
        )

    return one(left[0], right[0]) + (one(left[0], right[1]) + one(left[1], right[0]))


def kernel(
    devices, panels,
    p_hbm, t_hbm, later_hbm, out_ref,
    p_ref, t_ref, later_ref, p_high, p_low,
    y_ref, term, from_core, from_x, from_z, part_x, part_z, fan, send_w, got_w,
    in_sem, send_sem, y_sem, core_sem, x_sem, z_sem, fan_sem, w_sem,
):
    block, rhs = t_ref.shape
    levels = devices // PLANE
    piece = rhs // PLANE // SUBS
    group = rhs // GROUPS
    me = lax.axis_index("rows")
    level, q = me // PLANE, me % PLANE
    x, core = q // 2, q % 2
    mine = core * 2 + x
    facing = core * 2 + 1 - x
    sibling = me + 1 - 2 * core
    across = me + 2 - 4 * x
    up, down = me - PLANE, me + PLANE

    loads = {"t": pltpu.make_async_copy(t_hbm, t_ref, in_sem.at[0])}
    loads["later"] = pltpu.make_async_copy(later_hbm, later_ref, in_sem.at[1])
    for k in range(panels):
        loads[k] = pltpu.make_async_copy(
            p_hbm.at[:, k * block : (k + 1) * block], p_ref.at[k], in_sem.at[2 + k]
        )
    for name in ["t", 0, "later"] + list(range(panels - 1, 0, -1)):
        loads[name].start()

    barrier = pltpu.get_barrier_semaphore()
    for step in range(1, PLANE):
        other = level * PLANE + (q + step) % PLANE
        pl.semaphore_signal(barrier, inc=1, device_id={"rows": other}, device_id_type=MESH)

    @pl.when(level > 0)
    def _():
        pl.semaphore_signal(barrier, inc=1, device_id={"rows": up}, device_id_type=MESH)

    @pl.when(level < levels - 1)
    def _():
        pl.semaphore_signal(barrier, inc=1, device_id={"rows": down}, device_id_type=MESH)

    inner = jnp.logical_and(level > 0, level < levels - 1)

    def enter():
        @pl.when(inner)
        def _():
            pl.semaphore_wait(barrier, PLANE + 1)

        @pl.when(jnp.logical_not(inner))
        def _():
            pl.semaphore_wait(barrier, PLANE)

    class Sends:
        def __init__(self, me=None):
            self.held = []
            self.me = me

        def __call__(self, src, dst, recv, device, when=None):
            copy = pltpu.make_async_remote_copy(
                src_ref=src, dst_ref=dst, send_sem=send_sem.at[len(self.held)], recv_sem=recv,
                device_id={"rows": device}, device_id_type=MESH,
            )
            self.held.append((copy, when))
            if when is None:
                copy.start()
            else:
                pl.when(when)(copy.start)

        def finish(self):
            for copy, when in self.held:
                if when is None:
                    copy.wait_send()
                else:
                    pl.when(when)(copy.wait_send)

    def arrive(ref, sem):
        pltpu.make_async_remote_copy(
            src_ref=ref, dst_ref=ref, send_sem=send_sem.at[0], recv_sem=sem,
            device_id={"rows": sibling}, device_id_type=MESH,
        ).wait_recv()

    def send_y(send, k, at, h, device, when=None):
        send(y_ref.at[k, h, at], y_ref.at[k, h, at], y_sem.at[k, h, at], device, when)

    def wait_y(k, at, h):
        arrive(y_ref.at[k, h, at], y_sem.at[k, h, at])

    def y_value(k):
        return y_ref[k].reshape(rhs, block)

    def y_group(k, g):
        return y_ref[k, g].reshape(group, block)

    def fan_group(g):
        return fan[g].reshape(group, block)

    def store_y(k, g, value):
        y_ref[k, g] = value.reshape(PLANE, piece, block)

    def load_panel(k):
        loads[k].wait()
        high, low = split(p_ref[k])
        p_high[k] = high
        p_low[k] = low

    def panel(k):
        return p_high[k], p_low[k]

    def rows_of(g):
        return pl.ds(g * group, group)

    def relay(send, k, h):
        for side in range(2):
            at = core * 2 + side
            arrive(from_z.at[k, h, side], z_sem.at[k, h, side])
            value = from_z[k, h, side]
            if send.me == 3:
                value = value + term[k, h, at]
            else:
                arrive(from_x.at[k, h, side], x_sem.at[k, h, side])
                value = value + from_x[k, h, side]
            if send.me == k:
                fan[h, at] = value
            else:
                part_z[k, h, side] = value
                send(part_z.at[k, h, side], fan.at[h, at], fan_sem.at[h, at], k)

    def fan_wait(owner, h):
        other = 1 - owner % 2
        for at in (other * 2, other * 2 + 1):
            arrive(fan.at[h, at], fan_sem.at[h, at])

    def send_w_group(send, slot, to_slot, g, device):
        send(send_w.at[slot, rows_of(g)], got_w.at[to_slot, rows_of(g)], w_sem.at[to_slot, g], device)

    def wait_w(slot, g):
        arrive(got_w.at[slot, rows_of(g)], w_sem.at[slot, g])

    def drain(names):
        for name in names:
            loads[name].wait()

    @pl.when(me == 0)
    def _():
        send = Sends(0)
        loads["t"].wait()
        load_panel(0)
        target = t_ref[...].T
        for g in range(GROUPS):
            store_y(0, g, triple(split(target[g * group : (g + 1) * group]), panel(0), 1))
            if g == 0:
                enter()
            for at in range(PLANE):
                send_y(send, 0, at, g, 1)
                send_y(send, 0, at, g, 2)
                if at == 0:
                    send_y(send, 0, at, g, PLANE)
        drain(["later", 1, 2])
        for h in range(SUBS):
            wait_y(1, 0, h)
            send_y(send, 1, 0, h, PLANE)
        for h in range(SUBS):
            relay(send, 1, h)
        for h in range(SUBS):
            wait_y(2, 0, h)
            send_y(send, 2, 0, h, PLANE)
        for h in range(SUBS):
            relay(send, 0, h)
        for g in range(GROUPS):
            fan_wait(0, g)
            wait_w(0, g)
            right = y_group(0, g) - fan_group(g) - got_w[0, rows_of(g)]
            wait_w(1, g)
            answer = triple(split(right - got_w[1, rows_of(g)]), panel(0), 0)
            out_ref[:, g * group : (g + 1) * group] = answer.T
        send.finish()

    @pl.when(me == 1)
    def _():
        send = Sends(1)
        loads["t"].wait()
        target = t_ref[...].T
        load_panel(0)
        load_panel(1)
        enter()
        for g in range(GROUPS):
            for at in range(PLANE):
                wait_y(0, at, g)
                if at == 2:
                    send_y(send, 0, at, g, 1 + PLANE)
            right = target[g * group : (g + 1) * group] - triple(split(y_group(0, g)), panel(0), 1)
            store_y(1, g, triple(split(right), panel(1), 1))
            for at in range(PLANE):
                send_y(send, 1, at, g, 2)
                if at == 2:
                    send_y(send, 1, at, g, 1 + PLANE)
                if at == 0:
                    send_y(send, 1, at, g, 0)
        drain(["later", 2])
        for h in range(SUBS):
            relay(send, 1, h)
        for h in range(SUBS):
            wait_y(2, 2, h)
            send_y(send, 2, 2, h, 1 + PLANE)
        for h in range(SUBS):
            relay(send, 0, h)
        for g in range(GROUPS):
            fan_wait(1, g)
            right = y_group(1, g) - fan_group(g)
            wait_w(0, g)
            answer = triple(split(right - got_w[0, rows_of(g)]), panel(1), 0)
            send_w[0, rows_of(g)] = triple(split(answer), panel(0), 0)
            send_w_group(send, 0, 1, g, 0)
            out_ref[:, g * group : (g + 1) * group] = answer.T
        send.finish()

    @pl.when(me == 2)
    def _():
        send = Sends(2)
        loads["t"].wait()
        target = t_ref[...].T
        for k in range(panels):
            load_panel(k)
        enter()
        for g in range(GROUPS):
            right = target[g * group : (g + 1) * group]
            for k in range(2):
                for at in range(PLANE):
                    wait_y(k, at, g)
                    send_y(send, k, at, g, 3)
                    if at == 1:
                        send_y(send, k, at, g, 2 + PLANE)
                right = right - triple(split(y_group(k, g)), panel(k), 1)
            store_y(2, g, triple(split(right), panel(2), 1))
            for at in range(PLANE):
                if at == 0:
                    send_y(send, 2, at, g, 0)
                if at == 1:
                    send_y(send, 2, at, g, 2 + PLANE)
                if at == 2:
                    send_y(send, 2, at, g, 1)
                send_y(send, 2, at, g, 3)
        drain(["later"])
        for g in range(GROUPS):
            relay(send, 2, g)
            fan_wait(2, g)
            answer = triple(split(y_group(2, g) - fan_group(g)), panel(2), 0)
            send_w[0, rows_of(g)] = triple(split(answer), panel(1), 0)
            send_w_group(send, 0, 0, g, 1)
            send_w[1, rows_of(g)] = triple(split(answer), panel(0), 0)
            send_w_group(send, 1, 0, g, 0)
            out_ref[:, g * group : (g + 1) * group] = answer.T
        send.finish()

    @pl.when(me >= 3)
    def _():
        plane0 = level == 0
        loads["later"].wait()
        later = split(later_ref[...].T)

        def make_term(k):
            load_panel(k)
            term[k] = triple(later, panel(k), 0).reshape(SUBS, PLANE, piece, block)

        def subtract(k):
            value = triple(panel(k), split(y_value(k)), 1)
            out_ref[...] = (t_ref[...] if k == 0 else out_ref[...]) - value

        make_term(panels - 1)
        enter()

        @pl.when(plane0)
        def _():
            send = Sends(3)
            for k in range(panels - 1, -1, -1):
                if k < panels - 1:
                    make_term(k)
                for h in range(SUBS):
                    for at in range(PLANE):
                        device = k // 2 * 2 + at // 2
                        if device != 3:
                            send(
                                term.at[k, h, at], from_x.at[k, h, at % 2],
                                x_sem.at[k, h, at % 2], device,
                            )
            loads["t"].wait()

            def take(k):
                for h in range(SUBS):
                    for at in range(PLANE):
                        wait_y(k, at, h)
                        if at == 3:
                            send_y(send, k, at, h, 3 + PLANE)

            take(0)
            take(1)
            subtract(0)
            take(2)
            for h in range(SUBS):
                relay(send, 2, h)
            subtract(1)
            subtract(2)
            send.finish()

        @pl.when(jnp.logical_not(plane0))
        def _():
            far = level == levels - 1
            not_far = jnp.logical_not(far)
            send = Sends()
            for k in range(panels - 1, -1, -1):
                if k < panels - 1:
                    make_term(k)
                for h in range(SUBS):
                    for side in range(2):
                        send(
                            term.at[k, h, (1 - core) * 2 + side], from_core.at[k, h, side],
                            core_sem.at[k, h, side], sibling,
                        )
            loads["t"].wait()
            for k in range(panels - 1, -1, -1):
                for h in range(SUBS):
                    for side in range(2):
                        arrive(from_core.at[k, h, side], core_sem.at[k, h, side])
                        part_x[k, h, side] = term[k, h, core * 2 + side] + from_core[k, h, side]
                        send(
                            part_x.at[k, h, side], from_x.at[k, h, side],
                            x_sem.at[k, h, side], across, x != k // 2,
                        )

            def line_sum(k, send):
                here = x == k // 2
                for h in range(SUBS):
                    for side in range(2):

                        @pl.when(here)
                        def _():
                            arrive(from_x.at[k, h, side], x_sem.at[k, h, side])
                            part_z[k, h, side] = part_x[k, h, side] + from_x[k, h, side]

                        @pl.when(jnp.logical_and(here, not_far))
                        def _():
                            arrive(from_z.at[k, h, side], z_sem.at[k, h, side])
                            part_z[k, h, side] += from_z[k, h, side]

                        send(
                            part_z.at[k, h, side], from_z.at[k, h, side],
                            z_sem.at[k, h, side], up, here,
                        )

            def take(k, send):
                for h in range(SUBS):
                    wait_y(k, mine, h)
                    send_y(send, k, mine, h, down, not_far)
                    send_y(send, k, mine, h, across)
                    send_y(send, k, mine, h, sibling)

            def pass_on(k, send):
                for h in range(SUBS):
                    wait_y(k, facing, h)
                    send_y(send, k, facing, h, sibling)

            def rest(k):
                for h in range(SUBS):
                    for side in range(2):
                        wait_y(k, (1 - core) * 2 + side, h)

            def middle(order):
                inner_send = Sends()
                inner_send.held = list(send.held)
                done = len(send.held)
                for step, k in order:
                    step(k, inner_send)
                inner_send.held = inner_send.held[done:]
                inner_send.finish()

            last = [(pass_on, 0), (pass_on, 1)]
            steps = {
                "near": [(take, 0), (line_sum, 2), (take, 1), (line_sum, 1), (line_sum, 0)] + last,
                "far": [(line_sum, 2), (line_sum, 1), (line_sum, 0), (take, 0), (take, 1)] + last,
                "mid": [(line_sum, 2), (take, 0), (line_sum, 1), (take, 1), (line_sum, 0)] + last,
            }
            is_near = jnp.logical_and(level == 1, not_far)
            pl.when(is_near)(lambda: middle(steps["near"]))
            pl.when(far)(lambda: middle(steps["far"]))
            pl.when(jnp.logical_and(level > 1, not_far))(lambda: middle(steps["mid"]))
            for k in range(2):
                rest(k)
                subtract(k)
            take(2, send)
            pass_on(2, send)
            rest(2)
            subtract(2)
            send.finish()


def solution(mesh):
    devices = mesh.shape["rows"]

    def local(factor_panels, targets, later_solutions):
        block, rhs = targets.shape
        panels = factor_panels.shape[1] // block
        piece = rhs // PLANE // SUBS
        dma = pltpu.SemaphoreType.DMA
        f32 = jnp.float32
        return pl.pallas_call(
            functools.partial(kernel, devices, panels),
            out_shape=jax.ShapeDtypeStruct((block, rhs), f32),
            in_specs=[pl.BlockSpec(memory_space=pltpu.HBM)] * 3,
            out_specs=pl.BlockSpec(memory_space=pltpu.VMEM),
            scratch_shapes=[
                pltpu.VMEM((panels, block, block), f32),
                pltpu.VMEM((block, rhs), f32),
                pltpu.VMEM((block, rhs), f32),
                pltpu.VMEM((panels, block, block), jnp.bfloat16),
                pltpu.VMEM((panels, block, block), jnp.bfloat16),
                pltpu.VMEM((panels, SUBS, PLANE, piece, block), f32),
                pltpu.VMEM((panels, SUBS, PLANE, piece, block), f32),
                pltpu.VMEM((panels, SUBS, 2, piece, block), f32),
                pltpu.VMEM((panels, SUBS, 2, piece, block), f32),
                pltpu.VMEM((panels, SUBS, 2, piece, block), f32),
                pltpu.VMEM((panels, SUBS, 2, piece, block), f32),
                pltpu.VMEM((panels, SUBS, 2, piece, block), f32),
                pltpu.VMEM((SUBS, PLANE, piece, block), f32),
                pltpu.VMEM((2, rhs, block), f32),
                pltpu.VMEM((2, rhs, block), f32),
                dma((2 + panels,)),
                dma((256,)),
                dma((panels, SUBS, PLANE)),
                dma((panels, SUBS, 2)),
                dma((panels, SUBS, 2)),
                dma((panels, SUBS, 2)),
                dma((SUBS, PLANE)),
                dma((2, GROUPS)),
            ],
            compiler_params=pltpu.CompilerParams(
                collective_id=0, has_side_effects=True, vmem_limit_bytes=62 * 1024 * 1024
            ),
        )(factor_panels, targets, later_solutions)

    rows = P(("parts", "rows"), None)
    return jax.shard_map(
        local, mesh=mesh, in_specs=(rows, rows, rows), out_specs=rows, check_vma=False
    )
```

```python
import functools

import jax
import jax.numpy as jnp
from jax import lax
from jax.experimental import pallas as pl
from jax.experimental.pallas import tpu as pltpu
from jax.sharding import PartitionSpec as P

MESH = pl.DeviceIdType.MESH
PLANE = 4
SUBS = 4
GROUPS = SUBS
SHARED = 2


def split(value):
    high = value.astype(jnp.bfloat16)
    return high, (value - high.astype(jnp.float32)).astype(jnp.bfloat16)


def triple(left, right, contract):
    def one(a, b):
        return lax.dot_general(
            a, b, (((1,), (contract,)), ((), ())), preferred_element_type=jnp.float32
        )

    return one(left[0], right[0]) + (one(left[0], right[1]) + one(left[1], right[0]))


def kernel(
    devices, panels,
    p_hbm, t_hbm, later_hbm, out_ref,
    p_ref, t_ref, later_ref, p_high, p_low,
    y_ref, term, from_core, from_x, from_z, part_x, part_z, fan, send_w, got_w,
    in_sem, send_sem, y_sem, core_sem, x_sem, z_sem, fan_sem, w_sem,
):
    block, rhs = t_ref.shape
    levels = devices // PLANE
    piece = rhs // PLANE // SUBS
    group = rhs // GROUPS
    me = lax.axis_index("rows")
    level, q = me // PLANE, me % PLANE
    x, core = q // 2, q % 2
    mine = core * 2 + x
    facing = core * 2 + 1 - x
    sibling = me + 1 - 2 * core
    across = me + 2 - 4 * x
    up, down = me - PLANE, me + PLANE

    loads = {"t": pltpu.make_async_copy(t_hbm, t_ref, in_sem.at[0])}
    loads["later"] = pltpu.make_async_copy(later_hbm, later_ref, in_sem.at[1])
    for k in range(panels):
        loads[k] = pltpu.make_async_copy(
            p_hbm.at[:, k * block : (k + 1) * block], p_ref.at[k], in_sem.at[2 + k]
        )
    for name in ["t", 0, "later"] + list(range(panels - 1, 0, -1)):
        loads[name].start()

    barrier = pltpu.get_barrier_semaphore()
    for step in range(1, PLANE):
        other = level * PLANE + (q + step) % PLANE
        pl.semaphore_signal(barrier, inc=1, device_id={"rows": other}, device_id_type=MESH)

    @pl.when(level > 0)
    def _():
        pl.semaphore_signal(barrier, inc=1, device_id={"rows": up}, device_id_type=MESH)

    @pl.when(level < levels - 1)
    def _():
        pl.semaphore_signal(barrier, inc=1, device_id={"rows": down}, device_id_type=MESH)

    inner = jnp.logical_and(level > 0, level < levels - 1)

    def enter():
        @pl.when(inner)
        def _():
            pl.semaphore_wait(barrier, PLANE + 1)

        @pl.when(jnp.logical_not(inner))
        def _():
            pl.semaphore_wait(barrier, PLANE)

    class Sends:
        def __init__(self, me=None):
            self.held = []
            self.me = me

        def __call__(self, src, dst, recv, device, when=None):
            copy = pltpu.make_async_remote_copy(
                src_ref=src, dst_ref=dst, send_sem=send_sem.at[len(self.held)], recv_sem=recv,
                device_id={"rows": device}, device_id_type=MESH,
            )
            self.held.append((copy, when))
            if when is None:
                copy.start()
            else:
                pl.when(when)(copy.start)

        def finish(self):
            for copy, when in self.held:
                if when is None:
                    copy.wait_send()
                else:
                    pl.when(when)(copy.wait_send)

    def arrive(ref, sem):
        pltpu.make_async_remote_copy(
            src_ref=ref, dst_ref=ref, send_sem=send_sem.at[0], recv_sem=sem,
            device_id={"rows": sibling}, device_id_type=MESH,
        ).wait_recv()

    def send_y(send, k, at, h, device, when=None):
        send(y_ref.at[k, h, at], y_ref.at[k, h, at], y_sem.at[k, h, at], device, when)

    def wait_y(k, at, h):
        arrive(y_ref.at[k, h, at], y_sem.at[k, h, at])

    def y_value(k):
        return y_ref[k].reshape(rhs, block)

    def y_group(k, g):
        return y_ref[k, g].reshape(group, block)

    def fan_group(g):
        return fan[g].reshape(group, block)

    def store_y(k, g, value):
        y_ref[k, g] = value.reshape(PLANE, piece, block)

    def load_panel(k):
        loads[k].wait()
        high, low = split(p_ref[k])
        p_high[k] = high
        p_low[k] = low

    def panel(k):
        return p_high[k], p_low[k]

    def rows_of(g):
        return pl.ds(g * group, group)

    def relay(send, k, h):
        for side in range(1 if k == SHARED else 2):
            at = mine if k == SHARED else core * 2 + side
            arrive(from_z.at[k, h, side], z_sem.at[k, h, side])
            value = from_z[k, h, side]
            if send.me == 3:
                value = value + term[k, h, at]
            else:
                arrive(from_x.at[k, h, side], x_sem.at[k, h, side])
                value = value + from_x[k, h, side]
            if send.me == k:
                fan[h, at] = value
            else:
                part_z[k, h, side] = value
                send(part_z.at[k, h, side], fan.at[h, at], fan_sem.at[h, at], k)

    def fan_wait(owner, h):
        if owner == SHARED:
            others = [at for at in range(PLANE) if at != owner % 2 * 2 + owner // 2]
        else:
            others = [(1 - owner % 2) * 2, (1 - owner % 2) * 2 + 1]
        for at in others:
            arrive(fan.at[h, at], fan_sem.at[h, at])

    def send_w_group(send, slot, to_slot, g, device):
        send(send_w.at[slot, rows_of(g)], got_w.at[to_slot, rows_of(g)], w_sem.at[to_slot, g], device)

    def wait_w(slot, g):
        arrive(got_w.at[slot, rows_of(g)], w_sem.at[slot, g])

    def drain(names):
        for name in names:
            loads[name].wait()

    @pl.when(me == 0)
    def _():
        send = Sends(0)
        loads["t"].wait()
        load_panel(0)
        target = t_ref[...].T
        for g in range(GROUPS):
            store_y(0, g, triple(split(target[g * group : (g + 1) * group]), panel(0), 1))
            if g == 0:
                enter()
            for at in range(PLANE):
                send_y(send, 0, at, g, 1)
                send_y(send, 0, at, g, 2)
                if at == 0:
                    send_y(send, 0, at, g, PLANE)
        drain(["later", 1, 2])
        for h in range(SUBS):
            wait_y(1, 0, h)
            send_y(send, 1, 0, h, PLANE)
        for k in (2, 1):
            for h in range(SUBS):
                relay(send, k, h)
        for h in range(SUBS):
            wait_y(2, 0, h)
            send_y(send, 2, 0, h, PLANE)
        for h in range(SUBS):
            relay(send, 0, h)
        for g in range(GROUPS):
            fan_wait(0, g)
            wait_w(0, g)
            right = y_group(0, g) - fan_group(g) - got_w[0, rows_of(g)]
            wait_w(1, g)
            answer = triple(split(right - got_w[1, rows_of(g)]), panel(0), 0)
            out_ref[:, g * group : (g + 1) * group] = answer.T
        send.finish()

    @pl.when(me == 1)
    def _():
        send = Sends(1)
        loads["t"].wait()
        target = t_ref[...].T
        load_panel(0)
        load_panel(1)
        enter()
        for g in range(GROUPS):
            for at in range(PLANE):
                wait_y(0, at, g)
                if at == 2:
                    send_y(send, 0, at, g, 1 + PLANE)
            right = target[g * group : (g + 1) * group] - triple(split(y_group(0, g)), panel(0), 1)
            store_y(1, g, triple(split(right), panel(1), 1))
            for at in range(PLANE):
                send_y(send, 1, at, g, 2)
                if at == 2:
                    send_y(send, 1, at, g, 1 + PLANE)
                if at == 0:
                    send_y(send, 1, at, g, 0)
        drain(["later", 2])
        for k in (2, 1):
            for h in range(SUBS):
                relay(send, k, h)
        for h in range(SUBS):
            wait_y(2, 2, h)
            send_y(send, 2, 2, h, 1 + PLANE)
        for h in range(SUBS):
            relay(send, 0, h)
        for g in range(GROUPS):
            fan_wait(1, g)
            right = y_group(1, g) - fan_group(g)
            wait_w(0, g)
            answer = triple(split(right - got_w[0, rows_of(g)]), panel(1), 0)
            send_w[0, rows_of(g)] = triple(split(answer), panel(0), 0)
            send_w_group(send, 0, 1, g, 0)
            out_ref[:, g * group : (g + 1) * group] = answer.T
        send.finish()

    @pl.when(me == 2)
    def _():
        send = Sends(2)
        loads["t"].wait()
        target = t_ref[...].T
        for k in range(panels):
            load_panel(k)
        enter()
        for g in range(GROUPS):
            right = target[g * group : (g + 1) * group]
            for k in range(2):
                for at in range(PLANE):
                    wait_y(k, at, g)
                    send_y(send, k, at, g, 3)
                    if at == 1:
                        send_y(send, k, at, g, 2 + PLANE)
                right = right - triple(split(y_group(k, g)), panel(k), 1)
            store_y(2, g, triple(split(right), panel(2), 1))
            for at in range(PLANE):
                if at == 0:
                    send_y(send, 2, at, g, 0)
                if at == 1:
                    send_y(send, 2, at, g, 2 + PLANE)
                if at == 2:
                    send_y(send, 2, at, g, 1)
                send_y(send, 2, at, g, 3)
        drain(["later"])
        for g in range(GROUPS):
            relay(send, 2, g)
            fan_wait(2, g)
            answer = triple(split(y_group(2, g) - fan_group(g)), panel(2), 0)
            send_w[0, rows_of(g)] = triple(split(answer), panel(1), 0)
            send_w_group(send, 0, 0, g, 1)
            got_w[0, rows_of(g)] = answer
        for g in range(GROUPS):
            answer = got_w[0, rows_of(g)]
            send_w[1, rows_of(g)] = triple(split(answer), panel(0), 0)
            send_w_group(send, 1, 0, g, 0)
            out_ref[:, g * group : (g + 1) * group] = answer.T
        send.finish()

    @pl.when(me >= 3)
    def _():
        plane0 = level == 0
        loads["later"].wait()
        later = split(later_ref[...].T)

        def make_term(k):
            load_panel(k)
            term[k] = triple(later, panel(k), 0).reshape(SUBS, PLANE, piece, block)

        def subtract(k):
            value = triple(panel(k), split(y_value(k)), 1)
            out_ref[...] = (t_ref[...] if k == 0 else out_ref[...]) - value

        make_term(panels - 1)
        enter()

        @pl.when(plane0)
        def _():
            send = Sends(3)
            for k in range(panels - 1, -1, -1):
                if k < panels - 1:
                    make_term(k)
                for h in range(SUBS):
                    for at in range(PLANE):
                        device, slot = k // 2 * 2 + at // 2, at % 2
                        if k == SHARED:
                            device, slot = at % 2 * 2 + at // 2, 0
                        if device != 3:
                            send(
                                term.at[k, h, at], from_x.at[k, h, slot],
                                x_sem.at[k, h, slot], device,
                            )
            loads["t"].wait()

            def take(k):
                for h in range(SUBS):
                    for at in range(PLANE):
                        wait_y(k, at, h)
                        if at == 3:
                            send_y(send, k, at, h, 3 + PLANE)

            take(0)
            take(1)
            subtract(0)
            take(2)
            for h in range(SUBS):
                relay(send, 2, h)
            subtract(1)
            subtract(2)
            send.finish()

        @pl.when(jnp.logical_not(plane0))
        def _():
            far = level == levels - 1
            not_far = jnp.logical_not(far)
            send = Sends()
            for k in range(panels - 1, -1, -1):
                if k < panels - 1:
                    make_term(k)
                for h in range(SUBS):
                    for side in range(2):
                        send(
                            term.at[k, h, (1 - core) * 2 + side], from_core.at[k, h, side],
                            core_sem.at[k, h, side], sibling,
                        )
            loads["t"].wait()
            for k in range(panels - 1, -1, -1):
                for h in range(SUBS):
                    for side in range(2):
                        arrive(from_core.at[k, h, side], core_sem.at[k, h, side])
                    if k == SHARED:
                        part_x[k, h, 1] = term[k, h, facing] + from_core[k, h, 1 - x]
                        send(part_x.at[k, h, 1], from_x.at[k, h, 0], x_sem.at[k, h, 0], across)
                        part_x[k, h, 0] = term[k, h, mine] + from_core[k, h, x]
                        continue
                    for side in range(2):
                        part_x[k, h, side] = term[k, h, core * 2 + side] + from_core[k, h, side]
                        send(
                            part_x.at[k, h, side], from_x.at[k, h, side],
                            x_sem.at[k, h, side], across, x != k // 2,
                        )

            def line_sum(k, send):
                here = always if k == SHARED else at_x[k // 2]
                for h in range(SUBS):
                    for side in range(1 if k == SHARED else 2):

                        @pl.when(here)
                        def _():
                            arrive(from_x.at[k, h, side], x_sem.at[k, h, side])
                            part_z[k, h, side] = part_x[k, h, side] + from_x[k, h, side]

                        @pl.when(jnp.logical_and(here, not_far))
                        def _():
                            arrive(from_z.at[k, h, side], z_sem.at[k, h, side])
                            part_z[k, h, side] += from_z[k, h, side]

                        send(
                            part_z.at[k, h, side], from_z.at[k, h, side],
                            z_sem.at[k, h, side], up, here,
                        )

            def take(k, send):
                for h in range(SUBS):
                    wait_y(k, mine, h)
                    send_y(send, k, mine, h, down, not_far)
                    send_y(send, k, mine, h, across)
                    send_y(send, k, mine, h, sibling)

            def pass_on(k, send):
                for h in range(SUBS):
                    wait_y(k, facing, h)
                    send_y(send, k, facing, h, sibling)

            def rest(k):
                for h in range(SUBS):
                    for side in range(2):
                        wait_y(k, (1 - core) * 2 + side, h)

            middles = []
            at_x = [x == 0, x == 1]
            always = level > 0

            def sent(first, conditions):
                for index, when in enumerate(conditions):
                    wait = pltpu.make_async_remote_copy(
                        src_ref=part_z.at[0, 0, 0], dst_ref=part_z.at[0, 0, 0],
                        send_sem=send_sem.at[first + index], recv_sem=z_sem.at[0, 0, 0],
                        device_id={"rows": sibling}, device_id_type=MESH,
                    ).wait_send
                    if when is None:
                        wait()
                    else:
                        pl.when(when)(wait)

            def middle(order):
                inner_send = Sends()
                inner_send.held = list(send.held)
                done = len(send.held)
                for step, k in order:
                    step(k, inner_send)
                middles.append([when for _, when in inner_send.held[done:]])

            steps = {
                "near": [(take, 0), (line_sum, 2), (take, 1), (line_sum, 1), (pass_on, 0), (take, 2), (line_sum, 0)],
                "far": [(line_sum, 2), (line_sum, 1), (line_sum, 0), (take, 0), (take, 1), (pass_on, 0), (take, 2)],
                "mid": [(line_sum, 2), (take, 0), (line_sum, 1), (take, 1), (line_sum, 0), (pass_on, 0), (take, 2)],
            }
            is_near = jnp.logical_and(level == 1, not_far)
            is_mid = jnp.logical_and(level > 1, not_far)
            pl.when(is_near)(lambda: middle(steps["near"]))
            pl.when(far)(lambda: middle(steps["far"]))
            pl.when(is_mid)(lambda: middle(steps["mid"]))
            first = len(send.held)
            send.held += [None] * len(middles[0])
            pass_on(1, send)
            rest(0)
            subtract(0)
            rest(1)
            pass_on(2, send)
            subtract(1)
            rest(2)
            subtract(2)
            send.held = send.held[:first] + send.held[first + len(middles[0]) :]
            send.finish()
            for branch, conditions in zip((is_near, far, is_mid), middles):
                pl.when(branch)(functools.partial(sent, first, conditions))


def solution(mesh):
    devices = mesh.shape["rows"]

    def local(factor_panels, targets, later_solutions):
        block, rhs = targets.shape
        panels = factor_panels.shape[1] // block
        piece = rhs // PLANE // SUBS
        dma = pltpu.SemaphoreType.DMA
        f32 = jnp.float32
        return pl.pallas_call(
            functools.partial(kernel, devices, panels),
            out_shape=jax.ShapeDtypeStruct((block, rhs), f32),
            in_specs=[pl.BlockSpec(memory_space=pltpu.HBM)] * 3,
            out_specs=pl.BlockSpec(memory_space=pltpu.VMEM),
            scratch_shapes=[
                pltpu.VMEM((panels, block, block), f32),
                pltpu.VMEM((block, rhs), f32),
                pltpu.VMEM((block, rhs), f32),
                pltpu.VMEM((panels, block, block), jnp.bfloat16),
                pltpu.VMEM((panels, block, block), jnp.bfloat16),
                pltpu.VMEM((panels, SUBS, PLANE, piece, block), f32),
                pltpu.VMEM((panels, SUBS, PLANE, piece, block), f32),
                pltpu.VMEM((panels, SUBS, 2, piece, block), f32),
                pltpu.VMEM((panels, SUBS, 2, piece, block), f32),
                pltpu.VMEM((panels, SUBS, 2, piece, block), f32),
                pltpu.VMEM((panels, SUBS, 2, piece, block), f32),
                pltpu.VMEM((panels, SUBS, 2, piece, block), f32),
                pltpu.VMEM((SUBS, PLANE, piece, block), f32),
                pltpu.VMEM((2, rhs, block), f32),
                pltpu.VMEM((2, rhs, block), f32),
                dma((2 + panels,)),
                dma((256,)),
                dma((panels, SUBS, PLANE)),
                dma((panels, SUBS, 2)),
                dma((panels, SUBS, 2)),
                dma((panels, SUBS, 2)),
                dma((SUBS, PLANE)),
                dma((2, GROUPS)),
            ],
            compiler_params=pltpu.CompilerParams(
                collective_id=0, has_side_effects=True, vmem_limit_bytes=62 * 1024 * 1024
            ),
        )(factor_panels, targets, later_solutions)

    rows = P(("parts", "rows"), None)
    return jax.shard_map(
        local, mesh=mesh, in_specs=(rows, rows, rows), out_specs=rows, check_vma=False
    )
```
